32 devices in a mesh: row: 8 (over z, y), col: 4 (over x, core).
Axes of the slice: x: 2, y: 2, z: 4, core: 2. Of those that a mesh axis runs over, the one named last changes fastest.
Arguments:
- tile_values: bfloat16 [8, 4, 4, 256, 256], P('row', 'col'), may hold values from -0.125 to 0.125
- tile_row: int32 [8, 4, 4], P('row', 'col'), may hold values from 0 to 3
- tile_col: int32 [8, 4, 4], P('row', 'col'), may hold values from 0 to 7
- basis_init: bfloat16 [32, 8192], P(None, ('col', 'row')), may hold values from -6 to 6
Outputs:
- ritz_basis: float32 [32, 8192], P(None, ('col', 'row'))
- residual: float32 [32, 8192], P(None, ('col', 'row'))
- projected: float32 [32, 32], replicated
The draws below stay inside these ranges and needn't reach their ends.
Inputs may be any that keep to these rules, and one draw needn't show every extreme that they name: `tile_row`: coordinates may repeat within a pair of blocks; repeated tiles add. `tile_col`: coordinates may repeat within a pair of blocks; repeated tiles add.
All inputs are finite; a program needn't handle non-finite values.
Results may differ from the reference program's by a relative error of at most 0.013.
Values may be sent and summed in bfloat16 or wider, within the bound.
A program may use at most 64 MiB of HBM per device.

```python
import jax
import jax.numpy as jnp
from jax import lax

K = 32
TB = 256
TILES = 4
M = 256
ITERS = 1
N = 8192
N_ROW = 8
N_COL = 4


def plant(values, own_key, low, largest):
    longest = values.shape.index(max(values.shape))
    spots = []
    for shift in (0, 1):
        where = [jax.random.randint(jax.random.fold_in(own_key, axis), (), 0, length) for axis, length in enumerate(values.shape)]
        where[longest] = (where[longest] + shift) % values.shape[longest]
        spots.append(tuple(where))
    return values.at[spots[0]].set(low).at[spots[1]].set(largest)


def level_of(key, shape, split, low, top_value):
    factor_of = 1.0
    for dim, parts in split:
        heights = jax.random.uniform(jax.random.fold_in(jax.random.fold_in(key, 6), dim), (parts,), jnp.float32, low / len(split), top_value / len(split))
        factor_of = factor_of * jnp.repeat(jnp.exp(heights), shape[dim] // parts).reshape((-1,) + (1,) * (len(shape) - 1 - dim))
    return factor_of


def bell_draw(key, shape, width, reach, split=(), kind=jnp.bfloat16):
    drawn = width * jax.random.normal(key, shape, jnp.float32)
    if split:
        drawn = drawn * level_of(key, shape, split, -0.22, 0.18)
    return jnp.clip(drawn, -reach, reach).astype(kind)


def setup_inputs(seed: int = 0) -> dict:
    keys = jax.random.split(jax.random.key(seed), 5)
    tile_values = bell_draw(keys[0], (N_ROW, N_COL, TILES, TB, TB), (2 * TILES * TB * TB // M) ** -0.5, 0.125, ((0, 8), (1, 4)))
    tile_row = plant(jax.random.randint(keys[1], (N_ROW, N_COL, TILES), 0, N_COL * M // TB), jax.random.fold_in(keys[1], 1), 0, (N_COL * M // TB) - 1).astype(jnp.int32)
    tile_col = plant(jax.random.randint(keys[2], (N_ROW, N_COL, TILES), 0, N_ROW * M // TB), jax.random.fold_in(keys[2], 1), 0, (N_ROW * M // TB) - 1).astype(jnp.int32)
    basis_init = bell_draw(keys[3], (K, N), 1.0, 6.0, ((1, 32),))
    return dict(tile_values=tile_values, tile_row=tile_row, tile_col=tile_col, basis_init=basis_init)


def exact_dot(left, right):
    return jnp.dot(left, right, precision=lax.Precision.HIGHEST)

def bucket(contrib, index, slots):
    tile_size = contrib.shape[-1]
    onehot_table = (index[:, None] == jnp.arange(slots, dtype=jnp.int32)[None, :]).astype(contrib.dtype)
    summed = jnp.einsum('ktb,tn->knb', contrib, onehot_table, precision=lax.Precision.HIGHEST)
    return summed.reshape(contrib.shape[0], slots * tile_size)

def partials(tile_block, tile_rows, tile_cols, column_block, row_block):
    tile_size = tile_block.shape[-1]
    vector_count = column_block.shape[0]
    col_tiles = column_block.shape[1] // tile_size
    row_tiles = row_block.shape[1] // tile_size
    weights = tile_block.astype(jnp.float32)
    picked = column_block.reshape(vector_count, col_tiles, tile_size)[:, tile_cols].astype(jnp.float32)
    direct = jnp.einsum('ktj,tij->kti', picked, weights, precision=lax.Precision.HIGHEST)
    mirror_pick = row_block.reshape(vector_count, row_tiles, tile_size)[:, tile_rows].astype(jnp.float32)
    mirror = jnp.einsum('kti,tij->ktj', mirror_pick, weights, precision=lax.Precision.HIGHEST)
    direct_part = lax.optimization_barrier(bucket(direct, tile_rows, row_tiles).astype(jnp.bfloat16)).astype(jnp.float32)
    mirror_part = lax.optimization_barrier(bucket(mirror, tile_cols, col_tiles).astype(jnp.bfloat16)).astype(jnp.float32)
    return (direct_part, mirror_part)

def apply_hamiltonian(tile_values, tile_row, tile_col, vectors_bf):
    vector_count = vectors_bf.shape[0]
    blocked = vectors_bf.reshape(vector_count, N_COL, N_ROW, M)
    column_blocks = jnp.transpose(blocked, (1, 0, 2, 3)).reshape(N_COL, vector_count, N_ROW * M)

    def one_row(running, row_index):
        row_block = lax.dynamic_index_in_dim(blocked, row_index, 2, keepdims=False).reshape(vector_count, N_COL * M)
        tiles_here = lax.dynamic_index_in_dim(tile_values, row_index, 0, keepdims=False)
        rows_here = lax.dynamic_index_in_dim(tile_row, row_index, 0, keepdims=False)
        cols_here = lax.dynamic_index_in_dim(tile_col, row_index, 0, keepdims=False)
        direct_parts, mirror_parts = jax.vmap(partials, in_axes=(0, 0, 0, 0, None))(tiles_here, rows_here, cols_here, column_blocks, row_block)
        return (running + mirror_parts, jnp.sum(direct_parts, axis=0))
    mirror_sum, direct_rows = lax.scan(one_row, jnp.zeros((N_COL, vector_count, N_ROW * M), jnp.float32), jnp.arange(N_ROW, dtype=jnp.int32))
    direct_full = jnp.transpose(direct_rows.reshape(N_ROW, vector_count, N_COL, M), (1, 2, 0, 3))
    mirror_full = jnp.transpose(mirror_sum.reshape(N_COL, vector_count, N_ROW, M), (1, 0, 2, 3))
    return (direct_full + mirror_full).reshape(vector_count, N_COL * N_ROW * M)

def reference(tile_values, tile_row, tile_col, basis_init):
    total_rows = N_ROW * N_COL * M
    current = basis_init
    ritz_basis = basis_init.astype(jnp.float32)
    for iteration in range(ITERS):
        product_block = apply_hamiltonian(tile_values, tile_row, tile_col, current)
        gram_matrix = exact_dot(product_block, product_block.T) / total_rows
        factor = jnp.linalg.cholesky(gram_matrix)
        ritz_basis = lax.linalg.triangular_solve(factor, product_block, left_side=True, lower=True)
        current = ritz_basis.astype(jnp.bfloat16)
    product_block = apply_hamiltonian(tile_values, tile_row, tile_col, current)
    projected = exact_dot(ritz_basis, product_block.T) / total_rows
    residual = product_block - exact_dot(projected.T, ritz_basis)
    return (ritz_basis, residual, projected)
```

```python
import functools

import jax
import jax.numpy as jnp
from jax import lax
from jax.experimental import pallas as pl
from jax.experimental.pallas import tpu as pltpu
from jax.sharding import PartitionSpec as P

MESH = pl.DeviceIdType.MESH
F32 = jnp.float32
BF16 = jnp.bfloat16
NT = (((1,), (1,)), ((), ()))


def exact_dot(left, right):
    return jnp.dot(left, right, precision=lax.Precision.HIGHEST, preferred_element_type=F32)


def exact_dot_nt(left, right):
    return lax.dot_general(
        left, right, NT, precision=lax.Precision.HIGHEST, preferred_element_type=F32
    )


def offsets(size):
    return sorted(range(1, size), key=lambda d: -min(d, size - d))


def pack(square):
    k = square.shape[0]
    per = 128 // k
    rows = k // per
    return jnp.concatenate([square[i * rows : (i + 1) * rows] for i in range(per)], axis=1)


def unpack(packed, k):
    per = 128 // k
    return jnp.concatenate([packed[:, i * k : (i + 1) * k] for i in range(per)], axis=0)


def inverse_factor(gram):
    k = gram.shape[0]
    row_id = lax.broadcasted_iota(jnp.int32, (k, 2 * k), 0)
    eye = (
        lax.broadcasted_iota(jnp.int32, (k, k), 0) == lax.broadcasted_iota(jnp.int32, (k, k), 1)
    ).astype(F32)
    work = jnp.concatenate([gram, eye], axis=1)
    out = jnp.zeros((k, 2 * k), F32)
    for i in range(k):
        scale = lax.rsqrt(work[i : i + 1, i : i + 1])
        row = work[i : i + 1, :] * scale
        column = work[:, i : i + 1] * scale
        out = jnp.where(row_id == i, row, out)
        if i < k - 1:
            work = work - column * row
    return out[:, k:]


def kernel(
    n_row, n_col, total_rows,
    tiles_ref, trow_ref, tcol_ref, x_ref,
    ritz_ref, res_ref, proj_ref,
    col_x, row_x, y_bf, dir_out, mir_out, dir_in, mir_in, small_row, small_col,
    send_sem, recv_sem,
):
    my_row = lax.axis_index("row")
    my_col = lax.axis_index("col")
    tile_count = tiles_ref.shape[0]
    k = x_ref.shape[0]

    def row_peer(d):
        return (lax.rem(my_row + d, n_row), my_col)

    def col_peer(d):
        return (my_row, lax.rem(my_col + d, n_col))

    barrier = pltpu.get_barrier_semaphore()
    for d in range(1, n_row):
        pl.semaphore_signal(barrier, inc=1, device_id=row_peer(d), device_id_type=MESH)
    for d in range(1, n_col):
        pl.semaphore_signal(barrier, inc=1, device_id=col_peer(d), device_id_type=MESH)

    col_x[0, my_row] = x_ref[...]
    row_x[0, my_col] = x_ref[...]
    pl.semaphore_wait(barrier, n_row + n_col - 2)

    def send(src, dst, channel, peer):
        pltpu.make_async_remote_copy(
            src_ref=src, dst_ref=dst, send_sem=send_sem.at[channel], recv_sem=recv_sem.at[channel],
            device_id=peer, device_id_type=MESH,
        ).start()

    def wait_in(ref, channel):
        pltpu.make_async_copy(ref, ref, recv_sem.at[channel]).wait()

    def wait_out(ref, channel):
        pltpu.make_async_copy(ref, ref, send_sem.at[channel]).wait()

    def gather_start(src, p):
        for d in offsets(n_row):
            send(src, col_x.at[p, my_row], 4 * p, row_peer(d))
        for d in offsets(n_col):
            send(src, row_x.at[p, my_col], 4 * p + 1, col_peer(d))

    def gather_wait(p):
        wait_in(col_x.at[p, pl.ds(0, n_row - 1)], 4 * p)
        wait_in(row_x.at[p, pl.ds(0, n_col - 1)], 4 * p + 1)

    def small_start(p, which):
        if which == 0:
            for d in offsets(n_row):
                send(small_row.at[p, my_row], small_row.at[p, my_row], 8 + 2 * p, row_peer(d))
        else:
            for d in offsets(n_col):
                send(small_col.at[p, my_col], small_col.at[p, my_col], 9 + 2 * p, col_peer(d))

    def small_sum(p, which):
        ref, size = ((small_row, n_row), (small_col, n_col))[which]
        wait_in(ref.at[p, pl.ds(0, size - 1)], 8 + 2 * p + which)
        value = ref[p, 0]
        for i in range(1, size):
            value = value + ref[p, i]
        return value

    def products(p):
        direct, mirror, row_picks = [], [], []
        for t in range(tile_count):
            picked = col_x[p, tcol_ref[t]]
            direct.append(
                lax.dot_general(picked, tiles_ref[t], NT, preferred_element_type=F32)
            )
            row_pick = row_x[p, trow_ref[t]]
            row_picks.append(row_pick)
            mirror.append(jnp.dot(row_pick, tiles_ref[t], preferred_element_type=F32))
        return direct, mirror, row_picks

    def bucket(parts, index_ref, slot):
        value = None
        for t in range(tile_count):
            term = jnp.where(index_ref[t] == slot, parts[t], 0.0)
            value = term if value is None else value + term
        return value.astype(BF16)

    def scatter_start(p, direct, mirror):
        for n in range(n_row):
            mir_out[p, n] = bucket(mirror, tcol_ref, n)
        for d in offsets(n_row):
            peer = row_peer(d)
            send(mir_out.at[p, peer[0]], mir_in.at[p, d - 1], 4 * p + 2, peer)
        for n in range(n_col):
            dir_out[p, n] = bucket(direct, trow_ref, n)
        for d in offsets(n_col):
            peer = col_peer(d)
            send(dir_out.at[p, peer[1]], dir_in.at[p, d - 1], 4 * p + 3, peer)

    def scatter_sum(p):
        value = dir_out[p, my_col].astype(F32) + mir_out[p, my_row].astype(F32)
        wait_in(dir_in.at[p], 4 * p + 3)
        for i in range(n_col - 1):
            value = value + dir_in[p, i].astype(F32)
        wait_in(mir_in.at[p], 4 * p + 2)
        for i in range(n_row - 1):
            value = value + mir_in[p, i].astype(F32)
        return value

    gather_start(x_ref, 0)
    gather_wait(0)
    direct, mirror, _ = products(0)
    scatter_start(0, direct, mirror)
    image = scatter_sum(0)

    y_bf[...] = image.astype(BF16)
    gather_start(y_bf, 1)
    col_x[1, my_row] = y_bf[...]
    row_x[1, my_col] = y_bf[...]
    small_row[0, my_row] = pack(exact_dot_nt(image, image))
    small_start(0, 0)
    gather_wait(1)
    direct, mirror, row_picks = products(1)
    cross = None
    for t in range(tile_count):
        high = direct[t].astype(BF16)
        low = (direct[t] - high.astype(F32)).astype(BF16)
        for part in (high, low):
            term = lax.dot_general(row_picks[t], part, NT, preferred_element_type=F32)
            cross = term if cross is None else cross + term
    small_row[1, my_row] = pack(cross)
    small_start(1, 0)
    small_col[0, my_col] = small_sum(0, 0)
    small_start(0, 1)
    scatter_start(1, direct, mirror)
    gram = unpack(small_sum(0, 1), k) / total_rows
    small_col[1, my_col] = small_sum(1, 0)
    small_start(1, 1)
    inverse = inverse_factor(gram)
    ritz = exact_dot(inverse, image)
    ritz_ref[...] = ritz
    half = unpack(small_sum(1, 1), k) / total_rows
    half = exact_dot_nt(exact_dot(inverse, half), inverse)
    projected = half + half.T
    proj_ref[...] = projected
    last = scatter_sum(1)
    res_ref[...] = exact_dot(inverse, last) - exact_dot(projected, ritz)

    for p in range(2):
        wait_out(col_x.at[p, pl.ds(0, n_row - 1)], 4 * p)
        wait_out(row_x.at[p, pl.ds(0, n_col - 1)], 4 * p + 1)
        wait_out(mir_in.at[p], 4 * p + 2)
        wait_out(dir_in.at[p], 4 * p + 3)
        wait_out(small_row.at[p, pl.ds(0, n_row - 1)], 8 + 2 * p)
        wait_out(small_col.at[p, pl.ds(0, n_col - 1)], 9 + 2 * p)


def shards(n_row, n_col, tile_values, tile_row, tile_col, basis_init):
    k, m = basis_init.shape
    tiles = tile_values[0, 0]
    total_rows = m * n_row * n_col
    packed = (k * k // 128, 128)
    vmem = pl.BlockSpec(memory_space=pltpu.VMEM)
    smem = pl.BlockSpec(memory_space=pltpu.SMEM)
    return pl.pallas_call(
        functools.partial(kernel, n_row, n_col, total_rows),
        out_shape=(
            jax.ShapeDtypeStruct((k, m), F32),
            jax.ShapeDtypeStruct((k, m), F32),
            jax.ShapeDtypeStruct((k, k), F32),
        ),
        in_specs=[vmem, smem, smem, vmem],
        out_specs=(vmem, vmem, vmem),
        scratch_shapes=[
            pltpu.VMEM((2, n_row, k, m), BF16),
            pltpu.VMEM((2, n_col, k, m), BF16),
            pltpu.VMEM((k, m), BF16),
            pltpu.VMEM((2, n_col, k, m), BF16),
            pltpu.VMEM((2, n_row, k, m), BF16),
            pltpu.VMEM((2, n_col - 1, k, m), BF16),
            pltpu.VMEM((2, n_row - 1, k, m), BF16),
            pltpu.VMEM((2, n_row) + packed, F32),
            pltpu.VMEM((2, n_col) + packed, F32),
            pltpu.SemaphoreType.DMA((12,)),
            pltpu.SemaphoreType.DMA((12,)),
        ],
        compiler_params=pltpu.CompilerParams(
            collective_id=0, has_side_effects=True, vmem_limit_bytes=32 * 1024 * 1024
        ),
    )(tiles, tile_row[0, 0], tile_col[0, 0], basis_init)


def solution(mesh):
    return jax.shard_map(
        functools.partial(shards, mesh.shape["row"], mesh.shape["col"]),
        mesh=mesh,
        in_specs=(
            P("row", "col", None, None, None),
            P("row", "col", None),
            P("row", "col", None),
            P(None, ("col", "row")),
        ),
        out_specs=(P(None, ("col", "row")), P(None, ("col", "row")), P()),
        check_vma=False,
    )
```

```python
import functools

import jax
import jax.numpy as jnp
from jax import lax
from jax.experimental import pallas as pl
from jax.experimental.pallas import tpu as pltpu
from jax.sharding import PartitionSpec as P

VMEM_BYTES = 62 * 1024 * 1024
MESH = pl.DeviceIdType.MESH
F32 = jnp.float32
BF16 = jnp.bfloat16
NT = (((1,), (1,)), ((), ()))


def exact_dot(left, right):
    return jnp.dot(left, right, precision=lax.Precision.HIGHEST, preferred_element_type=F32)


def exact_dot_nt(left, right):
    return lax.dot_general(
        left, right, NT, precision=lax.Precision.HIGHEST, preferred_element_type=F32
    )


def offsets(size):
    return sorted(range(1, size), key=lambda d: -min(d, size - d))


def pack(square):
    k = square.shape[0]
    per = 128 // k
    rows = k // per
    return jnp.concatenate([square[i * rows : (i + 1) * rows] for i in range(per)], axis=1)


def unpack(packed, k):
    per = 128 // k
    return jnp.concatenate([packed[:, i * k : (i + 1) * k] for i in range(per)], axis=0)


def start_elimination(gram):
    k = gram.shape[0]
    eye = (
        lax.broadcasted_iota(jnp.int32, (k, k), 0) == lax.broadcasted_iota(jnp.int32, (k, k), 1)
    ).astype(F32)
    return jnp.concatenate([gram, eye], axis=1), jnp.zeros((k, 2 * k), F32)


def eliminate(work, out, first, last):
    k = work.shape[0]
    row_id = lax.broadcasted_iota(jnp.int32, (k, 2 * k), 0)
    for i in range(first, last):
        scale = lax.rsqrt(work[i : i + 1, i : i + 1])
        row = work[i : i + 1, :] * scale
        column = work[:, i : i + 1] * scale
        out = jnp.where(row_id == i, row, out)
        if i < k - 1:
            work = work - column * row
    return work, out


def kernel(
    n_row, n_col, total_rows,
    tiles_hbm, trow_hbm, tcol_hbm, x_hbm,
    ritz_hbm, res_hbm, proj_hbm,
    ritz_ref, res_ref, proj_ref, col_x0, col_x1, row_x0, row_x1, y_bf, dir_out, mir_out, dir_in, mir_in, small_row, small_col,
    tiles_ref, trow_ref, tcol_ref, send_sem, recv_sem, load_sem, store_sem,
):
    col_x, row_x = (col_x0, col_x1), (row_x0, row_x1)
    my_row = lax.axis_index("row")
    my_col = lax.axis_index("col")
    tile_count = tiles_ref.shape[0]
    k = x_hbm.shape[0]

    def row_peer(d):
        return (lax.rem(my_row + d, n_row), my_col)

    def col_peer(d):
        return (my_row, lax.rem(my_col + d, n_col))

    barrier = pltpu.get_barrier_semaphore()
    for d in range(1, n_row):
        pl.semaphore_signal(barrier, inc=1, device_id=row_peer(d), device_id_type=MESH)
    for d in range(1, n_col):
        pl.semaphore_signal(barrier, inc=1, device_id=col_peer(d), device_id_type=MESH)

    loads = [
        pltpu.make_async_copy(src, dst, load_sem.at[i])
        for i, (src, dst) in enumerate((
            (x_hbm, col_x[0].at[my_row]),
            (x_hbm, row_x[0].at[my_col]),
            (tcol_hbm, tcol_ref),
            (trow_hbm, trow_ref),
            (tiles_hbm, tiles_ref),
        ))
    ]
    for load in loads:
        load.start()
    stores = [
        pltpu.make_async_copy(src, dst, store_sem.at[i])
        for i, (src, dst) in enumerate(
            ((ritz_ref, ritz_hbm), (res_ref, res_hbm), (proj_ref, proj_hbm))
        )
    ]
    loads[0].wait()
    pl.semaphore_wait(barrier, n_row + n_col - 2)

    def send(src, dst, channel, peer):
        pltpu.make_async_remote_copy(
            src_ref=src, dst_ref=dst, send_sem=send_sem.at[channel], recv_sem=recv_sem.at[channel],
            device_id=peer, device_id_type=MESH,
        ).start()

    def wait_in(ref, channel):
        pltpu.make_async_copy(ref, ref, recv_sem.at[channel]).wait()

    def wait_out(ref, channel):
        pltpu.make_async_copy(ref, ref, send_sem.at[channel]).wait()

    def gather_start(src, p):
        for d in offsets(n_row):
            send(src, col_x[p].at[my_row], 4 * p, row_peer(d))
        for d in offsets(n_col):
            send(src, row_x[p].at[my_col], 4 * p + 1, col_peer(d))

    def gather_wait(p):
        wait_in(col_x[p].at[pl.ds(0, n_row - 1)], 4 * p)
        wait_in(row_x[p].at[pl.ds(0, n_col - 1)], 4 * p + 1)

    def small_start(p, which):
        if which == 0:
            for d in offsets(n_row):
                send(small_row.at[p, my_row], small_row.at[p, my_row], 8 + 2 * p, row_peer(d))
        else:
            for d in offsets(n_col):
                send(small_col.at[p, my_col], small_col.at[p, my_col], 9 + 2 * p, col_peer(d))

    def small_sum(p, which):
        ref, size = ((small_row, n_row), (small_col, n_col))[which]
        wait_in(ref.at[p, pl.ds(0, size - 1)], 8 + 2 * p + which)
        value = ref[p, 0]
        for i in range(1, size):
            value = value + ref[p, i]
        return value

    def bucket(parts, index_ref, slot):
        value = None
        for t in range(tile_count):
            term = jnp.where(index_ref[t] == slot, parts[t], 0.0)
            value = term if value is None else value + term
        return value.astype(BF16)

    def mirror_start(p):
        mirror = [
            jnp.dot(row_x[p][trow_ref[t]], tiles_ref[t], preferred_element_type=F32)
            for t in range(tile_count)
        ]
        for d in offsets(n_row):
            peer = row_peer(d)
            mir_out[p, d] = bucket(mirror, tcol_ref, peer[0])
            send(mir_out.at[p, d], mir_in.at[p, d - 1], 4 * p + 2, peer)
        mir_out[p, 0] = bucket(mirror, tcol_ref, my_row)

    def direct_start(p):
        direct = [
            lax.dot_general(col_x[p][tcol_ref[t]], tiles_ref[t], NT, preferred_element_type=F32)
            for t in range(tile_count)
        ]
        for d in offsets(n_col):
            peer = col_peer(d)
            dir_out[p, d] = bucket(direct, trow_ref, peer[1])
            send(dir_out.at[p, d], dir_in.at[p, d - 1], 4 * p + 3, peer)
        dir_out[p, 0] = bucket(direct, trow_ref, my_col)
        return direct

    def scatter_sum(p):
        value = dir_out[p, 0].astype(F32) + mir_out[p, 0].astype(F32)
        wait_in(dir_in.at[p], 4 * p + 3)
        for i in range(n_col - 1):
            value = value + dir_in[p, i].astype(F32)
        wait_in(mir_in.at[p], 4 * p + 2)
        for i in range(n_row - 1):
            value = value + mir_in[p, i].astype(F32)
        return value

    gather_start(col_x[0].at[my_row], 0)
    for load in loads[1:]:
        load.wait()
    gather_wait(0)
    mirror_start(0)
    direct_start(0)
    image = scatter_sum(0)

    y_bf[...] = image.astype(BF16)
    gather_start(y_bf, 1)
    col_x[1][my_row] = y_bf[...]
    row_x[1][my_col] = y_bf[...]
    small_col[0, my_col] = pack(exact_dot_nt(image, image))
    small_start(0, 1)
    small_row[0, my_row] = small_sum(0, 1)
    small_start(0, 0)
    gather_wait(1)
    mirror_start(1)
    direct = direct_start(1)
    cross = None
    for t in range(tile_count):
        row_pick = row_x[1][trow_ref[t]]
        high = direct[t].astype(BF16)
        low = (direct[t] - high.astype(F32)).astype(BF16)
        for part in (high, low):
            term = lax.dot_general(row_pick, part, NT, preferred_element_type=F32)
            cross = term if cross is None else cross + term
    small_col[1, my_col] = pack(cross)
    small_start(1, 1)
    work, out = start_elimination(unpack(small_sum(0, 0), k) / total_rows)
    work, out = eliminate(work, out, 0, k // 2)
    small_row[1, my_row] = small_sum(1, 1)
    small_start(1, 0)
    work, out = eliminate(work, out, k // 2, k)
    inverse = out[:, k:]
    ritz = exact_dot(inverse, image)
    ritz_ref[...] = ritz
    stores[0].start()
    half = unpack(small_sum(1, 0), k) / total_rows
    half = exact_dot_nt(exact_dot(inverse, half), inverse)
    projected = half + half.T
    proj_ref[...] = projected
    stores[2].start()
    expected = exact_dot(projected, ritz)
    last = scatter_sum(1)
    res_ref[...] = exact_dot(inverse, last) - expected
    stores[1].start()

    for p in range(2):
        wait_out(col_x[p].at[pl.ds(0, n_row - 1)], 4 * p)
        wait_out(row_x[p].at[pl.ds(0, n_col - 1)], 4 * p + 1)
        wait_out(mir_in.at[p], 4 * p + 2)
        wait_out(dir_in.at[p], 4 * p + 3)
        wait_out(small_row.at[p, pl.ds(0, n_row - 1)], 8 + 2 * p)
        wait_out(small_col.at[p, pl.ds(0, n_col - 1)], 9 + 2 * p)
    for store in stores:
        store.wait()


def write_out(*refs):
    count = (len(refs) - 1) // 2
    sems = refs[-1]
    copies = [
        pltpu.make_async_copy(refs[i], refs[count + i], sems.at[i]) for i in range(count)
    ]
    for copy in copies:
        copy.start()
    for copy in copies:
        copy.wait()


def shards(n_row, n_col, tile_values, tile_row, tile_col, basis_init):
    k, m = basis_init.shape
    tiles = tile_values[0, 0]
    total_rows = m * n_row * n_col
    packed = (k * k // 128, 128)
    hbm = pl.BlockSpec(memory_space=pltpu.HBM)
    out_shape = (
        jax.ShapeDtypeStruct((k, m), F32),
        jax.ShapeDtypeStruct((k, m), F32),
        jax.ShapeDtypeStruct((k, k), F32),
    )
    results = pl.pallas_call(
        functools.partial(kernel, n_row, n_col, total_rows),
        out_shape=out_shape,
        in_specs=[hbm] * 4,
        out_specs=(hbm,) * 3,
        scratch_shapes=[pltpu.VMEM(shape.shape, F32) for shape in out_shape]
        + [
            pltpu.VMEM((n_row, k, m), BF16),
            pltpu.VMEM((n_row, k, m), BF16),
            pltpu.VMEM((n_col, k, m), BF16),
            pltpu.VMEM((n_col, k, m), BF16),
            pltpu.VMEM((k, m), BF16),
            pltpu.VMEM((2, n_col, k, m), BF16),
            pltpu.VMEM((2, n_row, k, m), BF16),
            pltpu.VMEM((2, n_col - 1, k, m), BF16),
            pltpu.VMEM((2, n_row - 1, k, m), BF16),
            pltpu.VMEM((2, n_row) + packed, F32),
            pltpu.VMEM((2, n_col) + packed, F32),
            pltpu.VMEM(tiles.shape, BF16),
            pltpu.SMEM((tiles.shape[0],), jnp.int32),
            pltpu.SMEM((tiles.shape[0],), jnp.int32),
            pltpu.SemaphoreType.DMA((12,)),
            pltpu.SemaphoreType.DMA((12,)),
            pltpu.SemaphoreType.DMA((5,)),
            pltpu.SemaphoreType.DMA((3,)),
        ],
        compiler_params=pltpu.CompilerParams(
            collective_id=0, has_side_effects=True, vmem_limit_bytes=VMEM_BYTES
        ),
    )(tiles, tile_row[0, 0], tile_col[0, 0], basis_init)
    return pl.pallas_call(
        write_out,
        out_shape=out_shape,
        in_specs=[hbm] * 3,
        out_specs=(hbm,) * 3,
        scratch_shapes=[pltpu.SemaphoreType.DMA((3,))],
    )(*results)


def solution(mesh):
    return jax.shard_map(
        functools.partial(shards, mesh.shape["row"], mesh.shape["col"]),
        mesh=mesh,
        in_specs=(
            P("row", "col", None, None, None),
            P("row", "col", None),
            P("row", "col", None),
            P(None, ("col", "row")),
        ),
        out_specs=(P(None, ("col", "row")), P(None, ("col", "row")), P()),
        check_vma=False,
    )
```

```python
import functools

import jax
import jax.numpy as jnp
from jax import lax
from jax.experimental import pallas as pl
from jax.experimental.pallas import tpu as pltpu
from jax.sharding import PartitionSpec as P

VMEM_BYTES = 62 * 1024 * 1024
MESH = pl.DeviceIdType.MESH
F32 = jnp.float32
BF16 = jnp.bfloat16
NT = (((1,), (1,)), ((), ()))


def exact_dot(left, right):
    return jnp.dot(left, right, precision=lax.Precision.HIGHEST, preferred_element_type=F32)


def exact_dot_nt(left, right):
    return lax.dot_general(
        left, right, NT, precision=lax.Precision.HIGHEST, preferred_element_type=F32
    )


def offsets(size):
    return sorted(range(1, size), key=lambda d: -min(d, size - d))


def pack(square):
    k = square.shape[0]
    per = 128 // k
    rows = k // per
    return jnp.concatenate([square[i * rows : (i + 1) * rows] for i in range(per)], axis=1)


def unpack(packed, k):
    per = 128 // k
    return jnp.concatenate([packed[:, i * k : (i + 1) * k] for i in range(per)], axis=0)


def start_elimination(gram):
    k = gram.shape[0]
    eye = (
        lax.broadcasted_iota(jnp.int32, (k, k), 0) == lax.broadcasted_iota(jnp.int32, (k, k), 1)
    ).astype(F32)
    return jnp.concatenate([gram, eye], axis=1), jnp.zeros((k, 2 * k), F32)


def eliminate(work, out, first, last):
    k = work.shape[0]
    row_id = lax.broadcasted_iota(jnp.int32, (k, 2 * k), 0)
    for i in range(first, last):
        scale = lax.rsqrt(work[i : i + 1, i : i + 1])
        row = work[i : i + 1, :] * scale
        column = work[:, i : i + 1] * scale
        out = jnp.where(row_id == i, row, out)
        if i < k - 1:
            work = work - column * row
    return work, out


def kernel(
    n_row, n_col, total_rows,
    tiles_hbm, trow_hbm, tcol_hbm, x_hbm,
    ritz_hbm, res_hbm, proj_hbm,
    ritz_ref, res_ref, proj_ref, col_x0, col_x1, row_x0, row_x1, y_bf, dir_out, mir_out, dir_in, mir_in, small_row, small_col,
    tiles_ref, trow_ref, tcol_ref, send_sem, recv_sem, load_sem, store_sem,
):
    col_x, row_x = (col_x0, col_x1), (row_x0, row_x1)
    my_row = lax.axis_index("row")
    my_col = lax.axis_index("col")
    tile_count = tiles_ref.shape[0]
    k = x_hbm.shape[0]

    def row_peer(d):
        return (lax.rem(my_row + d, n_row), my_col)

    def col_peer(d):
        return (my_row, lax.rem(my_col + d, n_col))

    barrier = pltpu.get_barrier_semaphore()
    for d in range(1, n_row):
        pl.semaphore_signal(barrier, inc=1, device_id=row_peer(d), device_id_type=MESH)
    for d in range(1, n_col):
        pl.semaphore_signal(barrier, inc=1, device_id=col_peer(d), device_id_type=MESH)

    loads = [
        pltpu.make_async_copy(src, dst, load_sem.at[i])
        for i, (src, dst) in enumerate((
            (x_hbm, col_x[0].at[my_row]),
            (x_hbm, row_x[0].at[my_col]),
            (tcol_hbm, tcol_ref),
            (trow_hbm, trow_ref),
            (tiles_hbm, tiles_ref),
        ))
    ]
    for load in loads:
        load.start()
    stores = [
        pltpu.make_async_copy(src, dst, store_sem.at[i])
        for i, (src, dst) in enumerate(
            ((ritz_ref, ritz_hbm), (res_ref, res_hbm), (proj_ref, proj_hbm))
        )
    ]
    loads[0].wait()
    pl.semaphore_wait(barrier, n_row + n_col - 2)

    def send(src, dst, channel, peer):
        pltpu.make_async_remote_copy(
            src_ref=src, dst_ref=dst, send_sem=send_sem.at[channel], recv_sem=recv_sem.at[channel],
            device_id=peer, device_id_type=MESH,
        ).start()

    def wait_in(ref, channel):
        pltpu.make_async_copy(ref, ref, recv_sem.at[channel]).wait()

    def wait_out(ref, channel):
        pltpu.make_async_copy(ref, ref, send_sem.at[channel]).wait()

    def gather_start(src, p):
        for d in offsets(n_row):
            send(src, col_x[p].at[my_row], 4 * p, row_peer(d))
        for d in offsets(n_col):
            send(src, row_x[p].at[my_col], 4 * p + 1, col_peer(d))

    def gather_wait(p):
        wait_in(col_x[p].at[pl.ds(0, n_row - 1)], 4 * p)
        wait_in(row_x[p].at[pl.ds(0, n_col - 1)], 4 * p + 1)

    def small_start(p, which):
        if which == 0:
            for d in offsets(n_row):
                send(small_row.at[p, my_row], small_row.at[p, my_row], 8 + 2 * p, row_peer(d))
        else:
            for d in offsets(n_col):
                send(small_col.at[p, my_col], small_col.at[p, my_col], 9 + 2 * p, col_peer(d))

    def small_sum(p, which):
        ref, size = ((small_row, n_row), (small_col, n_col))[which]
        wait_in(ref.at[p, pl.ds(0, size - 1)], 8 + 2 * p + which)
        value = ref[p, 0]
        for i in range(1, size):
            value = value + ref[p, i]
        return value

    def bucket(parts, index_ref, slot):
        value = None
        for t in range(tile_count):
            term = jnp.where(index_ref[t] == slot, parts[t], 0.0)
            value = term if value is None else value + term
        return value.astype(BF16)

    def mirror_start(p):
        mirror = [
            jnp.dot(row_x[p][trow_ref[t]], tiles_ref[t], preferred_element_type=F32)
            for t in range(tile_count)
        ]
        for d in offsets(n_row):
            peer = row_peer(d)
            mir_out[p, d] = bucket(mirror, tcol_ref, peer[0])
            send(mir_out.at[p, d], mir_in.at[p, d - 1], 4 * p + 2, peer)
        mir_out[p, 0] = bucket(mirror, tcol_ref, my_row)

    def direct_products(p):
        return [
            lax.dot_general(col_x[p][tcol_ref[t]], tiles_ref[t], NT, preferred_element_type=F32)
            for t in range(tile_count)
        ]

    def direct_start(p, direct):
        for d in offsets(n_col):
            peer = col_peer(d)
            dir_out[p, d] = bucket(direct, trow_ref, peer[1])
            send(dir_out.at[p, d], dir_in.at[p, d - 1], 4 * p + 3, peer)
        dir_out[p, 0] = bucket(direct, trow_ref, my_col)

    def scatter_sum(p):
        value = dir_out[p, 0].astype(F32) + mir_out[p, 0].astype(F32)
        wait_in(dir_in.at[p], 4 * p + 3)
        for i in range(n_col - 1):
            value = value + dir_in[p, i].astype(F32)
        wait_in(mir_in.at[p], 4 * p + 2)
        for i in range(n_row - 1):
            value = value + mir_in[p, i].astype(F32)
        return value

    gather_start(col_x[0].at[my_row], 0)
    for load in loads[1:]:
        load.wait()
    gather_wait(0)
    mirror_start(0)
    direct_start(0, direct_products(0))
    image = scatter_sum(0)

    y_bf[...] = image.astype(BF16)
    gather_start(y_bf, 1)
    col_x[1][my_row] = y_bf[...]
    row_x[1][my_col] = y_bf[...]
    small_col[0, my_col] = pack(exact_dot_nt(image, image))
    small_start(0, 1)
    small_row[0, my_row] = small_sum(0, 1)
    small_start(0, 0)
    gather_wait(1)
    direct = direct_products(1)
    cross = None
    for t in range(tile_count):
        row_pick = row_x[1][trow_ref[t]]
        high = direct[t].astype(BF16)
        low = (direct[t] - high.astype(F32)).astype(BF16)
        for part in (high, low):
            term = lax.dot_general(row_pick, part, NT, preferred_element_type=F32)
            cross = term if cross is None else cross + term
    small_col[1, my_col] = pack(cross)
    small_start(1, 1)
    mirror_start(1)
    direct_start(1, direct)
    work, out = start_elimination(unpack(small_sum(0, 0), k) / total_rows)
    work, out = eliminate(work, out, 0, k // 4)
    small_row[1, my_row] = small_sum(1, 1)
    small_start(1, 0)
    work, out = eliminate(work, out, k // 4, k)
    inverse = out[:, k:]
    ritz = exact_dot(inverse, image)
    ritz_ref[...] = ritz
    stores[0].start()
    half = unpack(small_sum(1, 0), k) / total_rows
    half = exact_dot_nt(exact_dot(inverse, half), inverse)
    projected = half + half.T
    proj_ref[...] = projected
    stores[2].start()
    expected = exact_dot(projected, ritz)
    last = scatter_sum(1)
    res_ref[...] = exact_dot(inverse, last) - expected
    stores[1].start()

    for p in range(2):
        wait_out(col_x[p].at[pl.ds(0, n_row - 1)], 4 * p)
        wait_out(row_x[p].at[pl.ds(0, n_col - 1)], 4 * p + 1)
        wait_out(mir_in.at[p], 4 * p + 2)
        wait_out(dir_in.at[p], 4 * p + 3)
        wait_out(small_row.at[p, pl.ds(0, n_row - 1)], 8 + 2 * p)
        wait_out(small_col.at[p, pl.ds(0, n_col - 1)], 9 + 2 * p)
    for store in stores:
        store.wait()


def write_out(*refs):
    results, outputs, staged = refs[:3], refs[3:6], refs[6:9]
    load_sem, store_sem = refs[9:]
    loads = [
        pltpu.make_async_copy(results[i], staged[i], load_sem.at[i]) for i in range(3)
    ]
    stores = [
        pltpu.make_async_copy(staged[i], outputs[i], store_sem.at[i]) for i in range(3)
    ]
    for load in loads:
        load.start()
    for load, store in zip(loads, stores):
        load.wait()
        store.start()
    for store in stores:
        store.wait()


def shards(n_row, n_col, tile_values, tile_row, tile_col, basis_init):
    k, m = basis_init.shape
    tiles = tile_values[0, 0]
    total_rows = m * n_row * n_col
    packed = (k * k // 128, 128)
    hbm = pl.BlockSpec(memory_space=pltpu.HBM)
    out_shape = (
        jax.ShapeDtypeStruct((k, m), F32),
        jax.ShapeDtypeStruct((k, m), F32),
        jax.ShapeDtypeStruct((k, k), F32),
    )
    results = pl.pallas_call(
        functools.partial(kernel, n_row, n_col, total_rows),
        out_shape=out_shape,
        in_specs=[hbm] * 4,
        out_specs=(hbm,) * 3,
        scratch_shapes=[pltpu.VMEM(shape.shape, F32) for shape in out_shape]
        + [
            pltpu.VMEM((n_row, k, m), BF16),
            pltpu.VMEM((n_row, k, m), BF16),
            pltpu.VMEM((n_col, k, m), BF16),
            pltpu.VMEM((n_col, k, m), BF16),
            pltpu.VMEM((k, m), BF16),
            pltpu.VMEM((2, n_col, k, m), BF16),
            pltpu.VMEM((2, n_row, k, m), BF16),
            pltpu.VMEM((2, n_col - 1, k, m), BF16),
            pltpu.VMEM((2, n_row - 1, k, m), BF16),
            pltpu.VMEM((2, n_row) + packed, F32),
            pltpu.VMEM((2, n_col) + packed, F32),
            pltpu.VMEM(tiles.shape, BF16),
            pltpu.SMEM((tiles.shape[0],), jnp.int32),
            pltpu.SMEM((tiles.shape[0],), jnp.int32),
            pltpu.SemaphoreType.DMA((12,)),
            pltpu.SemaphoreType.DMA((12,)),
            pltpu.SemaphoreType.DMA((5,)),
            pltpu.SemaphoreType.DMA((3,)),
        ],
        compiler_params=pltpu.CompilerParams(
            collective_id=0, has_side_effects=True, vmem_limit_bytes=VMEM_BYTES
        ),
    )(tiles, tile_row[0, 0], tile_col[0, 0], basis_init)
    return pl.pallas_call(
        write_out,
        out_shape=out_shape,
        in_specs=[hbm] * 3,
        out_specs=(hbm,) * 3,
        scratch_shapes=[pltpu.VMEM(shape.shape, F32) for shape in out_shape]
        + [pltpu.SemaphoreType.DMA((3,)), pltpu.SemaphoreType.DMA((3,))],
    )(*results)


def solution(mesh):
    return jax.shard_map(
        functools.partial(shards, mesh.shape["row"], mesh.shape["col"]),
        mesh=mesh,
        in_specs=(
            P("row", "col", None, None, None),
            P("row", "col", None),
            P("row", "col", None),
            P(None, ("col", "row")),
        ),
        out_specs=(P(None, ("col", "row")), P(None, ("col", "row")), P()),
        check_vma=False,
    )
```

```python
import functools

import jax
import jax.numpy as jnp
from jax import lax
from jax.experimental import pallas as pl
from jax.experimental.pallas import tpu as pltpu
from jax.sharding import PartitionSpec as P

VMEM_BYTES = 62 * 1024 * 1024
MESH = pl.DeviceIdType.MESH
F32 = jnp.float32
BF16 = jnp.bfloat16
NT = (((1,), (1,)), ((), ()))


def exact_dot(left, right):
    return jnp.dot(left, right, precision=lax.Precision.HIGHEST, preferred_element_type=F32)


def exact_dot_nt(left, right):
    return lax.dot_general(
        left, right, NT, precision=lax.Precision.HIGHEST, preferred_element_type=F32
    )


def offsets(size):
    return sorted(range(1, size), key=lambda d: -min(d, size - d))


def pack(square):
    k = square.shape[0]
    per = 128 // k
    rows = k // per
    return jnp.concatenate([square[i * rows : (i + 1) * rows] for i in range(per)], axis=1)


def unpack(packed, k):
    per = 128 // k
    return jnp.concatenate([packed[:, i * k : (i + 1) * k] for i in range(per)], axis=0)


def start_elimination(gram):
    k = gram.shape[0]
    eye = (
        lax.broadcasted_iota(jnp.int32, (k, k), 0) == lax.broadcasted_iota(jnp.int32, (k, k), 1)
    ).astype(F32)
    return jnp.concatenate([gram, eye], axis=1), jnp.zeros((k, 2 * k), F32)


def eliminate(work, out, first, last):
    k = work.shape[0]
    row_id = lax.broadcasted_iota(jnp.int32, (k, 2 * k), 0)
    for i in range(first, last):
        scale = lax.rsqrt(work[i : i + 1, i : i + 1])
        row = work[i : i + 1, :] * scale
        column = work[:, i : i + 1] * scale
        out = jnp.where(row_id == i, row, out)
        if i < k - 1:
            work = work - column * row
    return work, out


def kernel(
    n_row, n_col, total_rows,
    tiles_hbm, trow_hbm, tcol_hbm, x_hbm,
    ritz_hbm, res_hbm, proj_hbm,
    ritz_ref, res_ref, proj_ref, col_x0, col_x1, row_x0, row_x1, y_bf, dir_out, mir_out, dir_in, mir_in, small_row, small_col,
    tiles_ref, trow_ref, tcol_ref, send_sem, recv_sem, load_sem, store_sem,
):
    col_x, row_x = (col_x0, col_x1), (row_x0, row_x1)
    my_row = lax.axis_index("row")
    my_col = lax.axis_index("col")
    tile_count = tiles_ref.shape[0]
    k = x_hbm.shape[0]

    def row_peer(d):
        return (lax.rem(my_row + d, n_row), my_col)

    def col_peer(d):
        return (my_row, lax.rem(my_col + d, n_col))

    barrier = pltpu.get_barrier_semaphore()
    for d in range(1, n_row):
        pl.semaphore_signal(barrier, inc=1, device_id=row_peer(d), device_id_type=MESH)
    for d in range(1, n_col):
        pl.semaphore_signal(barrier, inc=1, device_id=col_peer(d), device_id_type=MESH)

    loads = [
        pltpu.make_async_copy(src, dst, load_sem.at[i])
        for i, (src, dst) in enumerate((
            (x_hbm, col_x[0].at[my_row]),
            (x_hbm, row_x[0].at[my_col]),
            (tcol_hbm, tcol_ref),
            (trow_hbm, trow_ref),
            (tiles_hbm, tiles_ref),
        ))
    ]
    for load in loads:
        load.start()
    stores = [
        pltpu.make_async_copy(src, dst, store_sem.at[i])
        for i, (src, dst) in enumerate(
            ((ritz_ref, ritz_hbm), (res_ref, res_hbm), (proj_ref, proj_hbm))
        )
    ]
    loads[0].wait()
    pl.semaphore_wait(barrier, n_row + n_col - 2)

    def send(src, dst, channel, peer):
        pltpu.make_async_remote_copy(
            src_ref=src, dst_ref=dst, send_sem=send_sem.at[channel], recv_sem=recv_sem.at[channel],
            device_id=peer, device_id_type=MESH,
        ).start()

    def wait_in(ref, channel):
        pltpu.make_async_copy(ref, ref, recv_sem.at[channel]).wait()

    def wait_out(ref, channel):
        pltpu.make_async_copy(ref, ref, send_sem.at[channel]).wait()

    def gather_start(src, p):
        for d in offsets(n_row):
            send(src, col_x[p].at[my_row], 4 * p, row_peer(d))
        for d in offsets(n_col):
            send(src, row_x[p].at[my_col], 4 * p + 1, col_peer(d))

    def gather_wait(p):
        wait_in(col_x[p].at[pl.ds(0, n_row - 1)], 4 * p)
        wait_in(row_x[p].at[pl.ds(0, n_col - 1)], 4 * p + 1)

    def small_start(p, which):
        if which == 0:
            for d in offsets(n_row):
                send(small_row.at[p, my_row], small_row.at[p, my_row], 8 + 2 * p, row_peer(d))
        else:
            for d in offsets(n_col):
                send(small_col.at[p, my_col], small_col.at[p, my_col], 9 + 2 * p, col_peer(d))

    def small_sum(p, which):
        ref, size = ((small_row, n_row), (small_col, n_col))[which]
        wait_in(ref.at[p, pl.ds(0, size - 1)], 8 + 2 * p + which)
        value = ref[p, 0]
        for i in range(1, size):
            value = value + ref[p, i]
        return value

    def bucket(parts, index_ref, slot):
        value = None
        for t in range(tile_count):
            term = jnp.where(index_ref[t] == slot, parts[t], 0.0)
            value = term if value is None else value + term
        return value.astype(BF16)

    def mirror_start(p):
        mirror = [
            jnp.dot(row_x[p][trow_ref[t]], tiles_ref[t], preferred_element_type=F32)
            for t in range(tile_count)
        ]
        for d in offsets(n_row):
            peer = row_peer(d)
            mir_out[p, d] = bucket(mirror, tcol_ref, peer[0])
            send(mir_out.at[p, d], mir_in.at[p, d - 1], 4 * p + 2, peer)
        mir_out[p, 0] = bucket(mirror, tcol_ref, my_row)

    def direct_products(p):
        return [
            lax.dot_general(col_x[p][tcol_ref[t]], tiles_ref[t], NT, preferred_element_type=F32)
            for t in range(tile_count)
        ]

    def direct_start(p, direct):
        for d in offsets(n_col):
            peer = col_peer(d)
            dir_out[p, d] = bucket(direct, trow_ref, peer[1])
            send(dir_out.at[p, d], dir_in.at[p, d - 1], 4 * p + 3, peer)
        dir_out[p, 0] = bucket(direct, trow_ref, my_col)

    def scatter_sum(p):
        value = dir_out[p, 0].astype(F32) + mir_out[p, 0].astype(F32)
        wait_in(dir_in.at[p], 4 * p + 3)
        for i in range(n_col - 1):
            value = value + dir_in[p, i].astype(F32)
        wait_in(mir_in.at[p], 4 * p + 2)
        for i in range(n_row - 1):
            value = value + mir_in[p, i].astype(F32)
        return value

    gather_start(col_x[0].at[my_row], 0)
    for load in loads[1:]:
        load.wait()
    gather_wait(0)
    mirror_start(0)
    direct_start(0, direct_products(0))
    image = scatter_sum(0)

    y_bf[...] = image.astype(BF16)
    gather_start(y_bf, 1)
    col_x[1][my_row] = y_bf[...]
    row_x[1][my_col] = y_bf[...]
    small_col[0, my_col] = pack(exact_dot_nt(image, image))
    small_start(0, 1)
    small_row[0, my_row] = small_sum(0, 1)
    small_start(0, 0)
    gather_wait(1)
    direct = direct_products(1)
    cross = None
    for t in range(tile_count):
        row_pick = row_x[1][trow_ref[t]]
        high = direct[t].astype(BF16)
        low = (direct[t] - high.astype(F32)).astype(BF16)
        for part in (high, low):
            term = lax.dot_general(row_pick, part, NT, preferred_element_type=F32)
            cross = term if cross is None else cross + term
    small_col[1, my_col] = pack(cross)
    small_start(1, 1)
    work, out = start_elimination(unpack(small_sum(0, 0), k) / total_rows)
    work, out = eliminate(work, out, 0, k // 2)
    small_row[1, my_row] = small_sum(1, 1)
    small_start(1, 0)
    mirror_start(1)
    direct_start(1, direct)
    work, out = eliminate(work, out, k // 2, k)
    inverse = out[:, k:]
    ritz = exact_dot(inverse, image)
    ritz_ref[...] = ritz
    stores[0].start()
    half = unpack(small_sum(1, 0), k) / total_rows
    half = exact_dot_nt(exact_dot(inverse, half), inverse)
    projected = half + half.T
    proj_ref[...] = projected
    stores[2].start()
    expected = exact_dot(projected, ritz)
    last = scatter_sum(1)
    res_ref[...] = exact_dot(inverse, last) - expected
    stores[1].start()

    for p in range(2):
        wait_out(col_x[p].at[pl.ds(0, n_row - 1)], 4 * p)
        wait_out(row_x[p].at[pl.ds(0, n_col - 1)], 4 * p + 1)
        wait_out(mir_in.at[p], 4 * p + 2)
        wait_out(dir_in.at[p], 4 * p + 3)
        wait_out(small_row.at[p, pl.ds(0, n_row - 1)], 8 + 2 * p)
        wait_out(small_col.at[p, pl.ds(0, n_col - 1)], 9 + 2 * p)
    for store in stores:
        store.wait()


def write_out(*refs):
    results, outputs, staged = refs[:3], refs[3:6], refs[6:9]
    load_sem, store_sem = refs[9:]
    loads = [
        pltpu.make_async_copy(results[i], staged[i], load_sem.at[i]) for i in range(3)
    ]
    stores = [
        pltpu.make_async_copy(staged[i], outputs[i], store_sem.at[i]) for i in range(3)
    ]
    for load in loads:
        load.start()
    for load, store in zip(loads, stores):
        load.wait()
        store.start()
    for store in stores:
        store.wait()


def shards(n_row, n_col, tile_values, tile_row, tile_col, basis_init):
    k, m = basis_init.shape
    tiles = tile_values[0, 0]
    total_rows = m * n_row * n_col
    packed = (k * k // 128, 128)
    hbm = pl.BlockSpec(memory_space=pltpu.HBM)
    out_shape = (
        jax.ShapeDtypeStruct((k, m), F32),
        jax.ShapeDtypeStruct((k, m), F32),
        jax.ShapeDtypeStruct((k, k), F32),
    )
    results = pl.pallas_call(
        functools.partial(kernel, n_row, n_col, total_rows),
        out_shape=out_shape,
        in_specs=[hbm] * 4,
        out_specs=(hbm,) * 3,
        scratch_shapes=[pltpu.VMEM(shape.shape, F32) for shape in out_shape]
        + [
            pltpu.VMEM((n_row, k, m), BF16),
            pltpu.VMEM((n_row, k, m), BF16),
            pltpu.VMEM((n_col, k, m), BF16),
            pltpu.VMEM((n_col, k, m), BF16),
            pltpu.VMEM((k, m), BF16),
            pltpu.VMEM((2, n_col, k, m), BF16),
            pltpu.VMEM((2, n_row, k, m), BF16),
            pltpu.VMEM((2, n_col - 1, k, m), BF16),
            pltpu.VMEM((2, n_row - 1, k, m), BF16),
            pltpu.VMEM((2, n_row) + packed, F32),
            pltpu.VMEM((2, n_col) + packed, F32),
            pltpu.VMEM(tiles.shape, BF16),
            pltpu.SMEM((tiles.shape[0],), jnp.int32),
            pltpu.SMEM((tiles.shape[0],), jnp.int32),
            pltpu.SemaphoreType.DMA((12,)),
            pltpu.SemaphoreType.DMA((12,)),
            pltpu.SemaphoreType.DMA((5,)),
            pltpu.SemaphoreType.DMA((3,)),
        ],
        compiler_params=pltpu.CompilerParams(
            collective_id=0, has_side_effects=True, vmem_limit_bytes=VMEM_BYTES
        ),
    )(tiles, tile_row[0, 0], tile_col[0, 0], basis_init)
    return pl.pallas_call(
        write_out,
        out_shape=out_shape,
        in_specs=[hbm] * 3,
        out_specs=(hbm,) * 3,
        scratch_shapes=[pltpu.VMEM(shape.shape, F32) for shape in out_shape]
        + [pltpu.SemaphoreType.DMA((3,)), pltpu.SemaphoreType.DMA((3,))],
    )(*results)


def solution(mesh):
    return jax.shard_map(
        functools.partial(shards, mesh.shape["row"], mesh.shape["col"]),
        mesh=mesh,
        in_specs=(
            P("row", "col", None, None, None),
            P("row", "col", None),
            P("row", "col", None),
            P(None, ("col", "row")),
        ),
        out_specs=(P(None, ("col", "row")), P(None, ("col", "row")), P()),
        check_vma=False,
    )
```

```python
import functools

import jax
import jax.numpy as jnp
from jax import lax
from jax.experimental import pallas as pl
from jax.experimental.pallas import tpu as pltpu
from jax.sharding import PartitionSpec as P

VMEM_BYTES = 62 * 1024 * 1024
MESH = pl.DeviceIdType.MESH
F32 = jnp.float32
BF16 = jnp.bfloat16
NT = (((1,), (1,)), ((), ()))


def exact_dot(left, right):
    return jnp.dot(left, right, precision=lax.Precision.HIGHEST, preferred_element_type=F32)


def exact_dot_nt(left, right):
    return lax.dot_general(
        left, right, NT, precision=lax.Precision.HIGHEST, preferred_element_type=F32
    )


def offsets(size):
    return sorted(range(1, size), key=lambda d: min(d, size - d))


def pack(square):
    k = square.shape[0]
    per = 128 // k
    rows = k // per
    return jnp.concatenate([square[i * rows : (i + 1) * rows] for i in range(per)], axis=1)


def unpack(packed, k):
    per = 128 // k
    return jnp.concatenate([packed[:, i * k : (i + 1) * k] for i in range(per)], axis=0)


def start_elimination(gram):
    k = gram.shape[0]
    eye = (
        lax.broadcasted_iota(jnp.int32, (k, k), 0) == lax.broadcasted_iota(jnp.int32, (k, k), 1)
    ).astype(F32)
    return jnp.concatenate([gram, eye], axis=1), jnp.zeros((k, 2 * k), F32)


def eliminate(work, out, first, last):
    k = work.shape[0]
    row_id = lax.broadcasted_iota(jnp.int32, (k, 2 * k), 0)
    for i in range(first, last):
        scale = lax.rsqrt(work[i : i + 1, i : i + 1])
        row = work[i : i + 1, :] * scale
        column = work[:, i : i + 1] * scale
        out = jnp.where(row_id == i, row, out)
        if i < k - 1:
            work = work - column * row
    return work, out


def kernel(
    n_row, n_col, total_rows,
    tiles_hbm, trow_hbm, tcol_hbm, x_hbm,
    ritz_hbm, res_hbm, proj_hbm,
    ritz_ref, res_ref, proj_ref, col_x0, col_x1, row_x0, row_x1, y_bf, dir_out, mir_out, dir_in, mir_in, small_row, small_col,
    tiles_ref, trow_ref, tcol_ref, send_sem, recv_sem, load_sem, store_sem,
):
    col_x, row_x = (col_x0, col_x1), (row_x0, row_x1)
    my_row = lax.axis_index("row")
    my_col = lax.axis_index("col")
    tile_count = tiles_ref.shape[0]
    k = x_hbm.shape[0]

    def row_peer(d):
        return (lax.rem(my_row + d, n_row), my_col)

    def col_peer(d):
        return (my_row, lax.rem(my_col + d, n_col))

    barrier = pltpu.get_barrier_semaphore()
    for d in range(1, n_row):
        pl.semaphore_signal(barrier, inc=1, device_id=row_peer(d), device_id_type=MESH)
    for d in range(1, n_col):
        pl.semaphore_signal(barrier, inc=1, device_id=col_peer(d), device_id_type=MESH)

    loads = [
        pltpu.make_async_copy(src, dst, load_sem.at[i])
        for i, (src, dst) in enumerate((
            (x_hbm, col_x[0].at[my_row]),
            (x_hbm, row_x[0].at[my_col]),
            (tcol_hbm, tcol_ref),
            (trow_hbm, trow_ref),
            (tiles_hbm, tiles_ref),
        ))
    ]
    for load in loads:
        load.start()
    stores = [
        pltpu.make_async_copy(src, dst, store_sem.at[i])
        for i, (src, dst) in enumerate(
            ((ritz_ref, ritz_hbm), (res_ref, res_hbm), (proj_ref, proj_hbm))
        )
    ]
    loads[0].wait()
    pl.semaphore_wait(barrier, n_row + n_col - 2)

    def send(src, dst, channel, peer):
        pltpu.make_async_remote_copy(
            src_ref=src, dst_ref=dst, send_sem=send_sem.at[channel], recv_sem=recv_sem.at[channel],
            device_id=peer, device_id_type=MESH,
        ).start()

    def wait_in(ref, channel):
        pltpu.make_async_copy(ref, ref, recv_sem.at[channel]).wait()

    def wait_out(ref, channel):
        pltpu.make_async_copy(ref, ref, send_sem.at[channel]).wait()

    def gather_start(src, p):
        for d in offsets(n_row):
            send(src, col_x[p].at[my_row], 4 * p, row_peer(d))
        for d in offsets(n_col):
            send(src, row_x[p].at[my_col], 4 * p + 1, col_peer(d))

    def gather_wait(p):
        wait_in(col_x[p].at[pl.ds(0, n_row - 1)], 4 * p)
        wait_in(row_x[p].at[pl.ds(0, n_col - 1)], 4 * p + 1)

    def small_start(p, which):
        if which == 0:
            for d in offsets(n_row):
                send(small_row.at[p, my_row], small_row.at[p, my_row], 8 + 2 * p, row_peer(d))
        else:
            for d in offsets(n_col):
                send(small_col.at[p, my_col], small_col.at[p, my_col], 9 + 2 * p, col_peer(d))

    def small_sum(p, which):
        ref, size = ((small_row, n_row), (small_col, n_col))[which]
        wait_in(ref.at[p, pl.ds(0, size - 1)], 8 + 2 * p + which)
        value = ref[p, 0]
        for i in range(1, size):
            value = value + ref[p, i]
        return value

    def bucket(parts, index_ref, slot):
        value = None
        for t in range(tile_count):
            term = jnp.where(index_ref[t] == slot, parts[t], 0.0)
            value = term if value is None else value + term
        return value.astype(BF16)

    def mirror_start(p):
        mirror = [
            jnp.dot(row_x[p][trow_ref[t]], tiles_ref[t], preferred_element_type=F32)
            for t in range(tile_count)
        ]
        for d in offsets(n_row):
            peer = row_peer(d)
            mir_out[p, d] = bucket(mirror, tcol_ref, peer[0])
            send(mir_out.at[p, d], mir_in.at[p, d - 1], 4 * p + 2, peer)
        mir_out[p, 0] = bucket(mirror, tcol_ref, my_row)

    def direct_products(p):
        return [
            lax.dot_general(col_x[p][tcol_ref[t]], tiles_ref[t], NT, preferred_element_type=F32)
            for t in range(tile_count)
        ]

    def direct_start(p, direct):
        for d in offsets(n_col):
            peer = col_peer(d)
            dir_out[p, d] = bucket(direct, trow_ref, peer[1])
            send(dir_out.at[p, d], dir_in.at[p, d - 1], 4 * p + 3, peer)
        dir_out[p, 0] = bucket(direct, trow_ref, my_col)

    def scatter_sum(p):
        value = dir_out[p, 0].astype(F32) + mir_out[p, 0].astype(F32)
        wait_in(dir_in.at[p], 4 * p + 3)
        for i in range(n_col - 1):
            value = value + dir_in[p, i].astype(F32)
        wait_in(mir_in.at[p], 4 * p + 2)
        for i in range(n_row - 1):
            value = value + mir_in[p, i].astype(F32)
        return value

    gather_start(col_x[0].at[my_row], 0)
    for load in loads[1:]:
        load.wait()
    gather_wait(0)
    mirror_start(0)
    direct_start(0, direct_products(0))
    image = scatter_sum(0)

    y_bf[...] = image.astype(BF16)
    gather_start(y_bf, 1)
    col_x[1][my_row] = y_bf[...]
    row_x[1][my_col] = y_bf[...]
    small_col[0, my_col] = pack(exact_dot_nt(image, image))
    small_start(0, 1)
    small_row[0, my_row] = small_sum(0, 1)
    small_start(0, 0)
    gather_wait(1)
    direct = direct_products(1)
    cross = None
    for t in range(tile_count):
        row_pick = row_x[1][trow_ref[t]]
        high = direct[t].astype(BF16)
        low = (direct[t] - high.astype(F32)).astype(BF16)
        for part in (high, low):
            term = lax.dot_general(row_pick, part, NT, preferred_element_type=F32)
            cross = term if cross is None else cross + term
    small_col[1, my_col] = pack(cross)
    small_start(1, 1)
    mirror_start(1)
    direct_start(1, direct)
    work, out = start_elimination(unpack(small_sum(0, 0), k) / total_rows)
    work, out = eliminate(work, out, 0, k // 4)
    small_row[1, my_row] = small_sum(1, 1)
    small_start(1, 0)
    work, out = eliminate(work, out, k // 4, k)
    inverse = out[:, k:]
    ritz = exact_dot(inverse, image)
    ritz_ref[...] = ritz
    stores[0].start()
    half = unpack(small_sum(1, 0), k) / total_rows
    half = exact_dot_nt(exact_dot(inverse, half), inverse)
    projected = half + half.T
    proj_ref[...] = projected
    stores[2].start()
    expected = exact_dot(projected, ritz)
    last = scatter_sum(1)
    res_ref[...] = exact_dot(inverse, last) - expected
    stores[1].start()

    for p in range(2):
        wait_out(col_x[p].at[pl.ds(0, n_row - 1)], 4 * p)
        wait_out(row_x[p].at[pl.ds(0, n_col - 1)], 4 * p + 1)
        wait_out(mir_in.at[p], 4 * p + 2)
        wait_out(dir_in.at[p], 4 * p + 3)
        wait_out(small_row.at[p, pl.ds(0, n_row - 1)], 8 + 2 * p)
        wait_out(small_col.at[p, pl.ds(0, n_col - 1)], 9 + 2 * p)
    for store in stores:
        store.wait()


def write_out(*refs):
    results, outputs, staged = refs[:3], refs[3:6], refs[6:9]
    load_sem, store_sem = refs[9:]
    loads = [
        pltpu.make_async_copy(results[i], staged[i], load_sem.at[i]) for i in range(3)
    ]
    stores = [
        pltpu.make_async_copy(staged[i], outputs[i], store_sem.at[i]) for i in range(3)
    ]
    for load in loads:
        load.start()
    for load, store in zip(loads, stores):
        load.wait()
        store.start()
    for store in stores:
        store.wait()


def shards(n_row, n_col, tile_values, tile_row, tile_col, basis_init):
    k, m = basis_init.shape
    tiles = tile_values[0, 0]
    total_rows = m * n_row * n_col
    packed = (k * k // 128, 128)
    hbm = pl.BlockSpec(memory_space=pltpu.HBM)
    out_shape = (
        jax.ShapeDtypeStruct((k, m), F32),
        jax.ShapeDtypeStruct((k, m), F32),
        jax.ShapeDtypeStruct((k, k), F32),
    )
    results = pl.pallas_call(
        functools.partial(kernel, n_row, n_col, total_rows),
        out_shape=out_shape,
        in_specs=[hbm] * 4,
        out_specs=(hbm,) * 3,
        scratch_shapes=[pltpu.VMEM(shape.shape, F32) for shape in out_shape]
        + [
            pltpu.VMEM((n_row, k, m), BF16),
            pltpu.VMEM((n_row, k, m), BF16),
            pltpu.VMEM((n_col, k, m), BF16),
            pltpu.VMEM((n_col, k, m), BF16),
            pltpu.VMEM((k, m), BF16),
            pltpu.VMEM((2, n_col, k, m), BF16),
            pltpu.VMEM((2, n_row, k, m), BF16),
            pltpu.VMEM((2, n_col - 1, k, m), BF16),
            pltpu.VMEM((2, n_row - 1, k, m), BF16),
            pltpu.VMEM((2, n_row) + packed, F32),
            pltpu.VMEM((2, n_col) + packed, F32),
            pltpu.VMEM(tiles.shape, BF16),
            pltpu.SMEM((tiles.shape[0],), jnp.int32),
            pltpu.SMEM((tiles.shape[0],), jnp.int32),
            pltpu.SemaphoreType.DMA((12,)),
            pltpu.SemaphoreType.DMA((12,)),
            pltpu.SemaphoreType.DMA((5,)),
            pltpu.SemaphoreType.DMA((3,)),
        ],
        compiler_params=pltpu.CompilerParams(
            collective_id=0, has_side_effects=True, vmem_limit_bytes=VMEM_BYTES
        ),
    )(tiles, tile_row[0, 0], tile_col[0, 0], basis_init)
    return pl.pallas_call(
        write_out,
        out_shape=out_shape,
        in_specs=[hbm] * 3,
        out_specs=(hbm,) * 3,
        scratch_shapes=[pltpu.VMEM(shape.shape, F32) for shape in out_shape]
        + [pltpu.SemaphoreType.DMA((3,)), pltpu.SemaphoreType.DMA((3,))],
    )(*results)


def solution(mesh):
    return jax.shard_map(
        functools.partial(shards, mesh.shape["row"], mesh.shape["col"]),
        mesh=mesh,
        in_specs=(
            P("row", "col", None, None, None),
            P("row", "col", None),
            P("row", "col", None),
            P(None, ("col", "row")),
        ),
        out_specs=(P(None, ("col", "row")), P(None, ("col", "row")), P()),
        check_vma=False,
    )
```
